32 devices in a mesh: dp: 2 (over y), expert: 16 (over z, x, core).
Axes of the slice: x: 2, y: 2, z: 4, core: 2. Of those that a mesh axis runs over, the one named last changes fastest.
Arguments:
- tokens: bfloat16 [4096, 3584], P(('dp', 'expert')), may hold values from -6 to 6
- cotangent: bfloat16 [4096, 3584], P(('dp', 'expert')), may hold values from -0.59765625 to 0.59765625
- route_ids: int32 [4096, 8], P(('dp', 'expert')), may hold values from 0 to 383, as said below
- gates: bfloat16 [4096, 8], P(('dp', 'expert')), may hold values from 0.099609375 to 1
- w_gate: bfloat16 [16, 3584, 128], P('expert', None, 'dp'), may hold values from -0.09375 to 0.09375
- w_up: bfloat16 [16, 3584, 128], P('expert', None, 'dp'), may hold values from -0.09375 to 0.09375
- w_down: bfloat16 [16, 3584, 128], P('expert', None, 'dp'), may hold values from -0.125 to 0.125
Outputs:
- relaid_gate: bfloat16 [16, 3584, 128], P('expert', 'dp')
- relaid_up: bfloat16 [16, 3584, 128], P('expert', 'dp')
- relaid_down: bfloat16 [16, 3584, 128], P('expert', 'dp')
- grad_gate: float32 [16, 3584, 128], P('expert', 'dp')
- grad_up: float32 [16, 3584, 128], P('expert', 'dp')
- grad_down: float32 [16, 3584, 128], P('expert', 'dp')
- token_grad: bfloat16 [4096, 3584], P(('dp', 'expert'))
- gate_grad: float32 [4096, 8], P(('dp', 'expert'))
The draws below stay inside these ranges and needn't reach their ends.
Inputs may be any that keep to these rules, and one draw needn't show every extreme that they name: `route_ids`: each row names 8 different experts. Among the 128 rows of one device, at most 6 routes name any one expert below 1; on every device of one index of dp, one same expert below 1 is named by exactly 6 routes.
All inputs are finite; a program needn't handle non-finite values.
Results may differ from the reference program's by a relative error of at most 0.02.
Values may be sent and summed in bfloat16 or wider, within the bound.
A program may use at most 128 MiB of HBM per device.

```python
import jax
import jax.numpy as jnp
from jax import lax

D = 3584
HID = 2048
ALL_EXP = 384
TOPK = 8
HSPLIT = 16
CAP = 6
TOK_DEV = 128
HDEV = 128
SLABS = 16
EXPERTS = 1
TOKENS = 4096
N_DP = 2


def draw_route_ids(key, part):
    blocks = TOKENS // TOK_DEV
    rows_dp = blocks // SLABS
    subkeys = jax.random.split(key, 6)
    hot_row = jax.random.randint(subkeys[0], (rows_dp,), 0, EXPERTS)
    hot_expert = jnp.repeat(hot_row, SLABS)
    counts = jax.random.randint(subkeys[1], (blocks, EXPERTS), 0, CAP // 2 + 2)
    counts = jnp.where(jnp.arange(EXPERTS)[None, :] == hot_expert[:, None], CAP, counts)
    shuffle_keys = jax.random.split(subkeys[2], blocks * EXPERTS)
    shuffles = jax.vmap(lambda one_key: jax.random.permutation(one_key, TOK_DEV))(shuffle_keys)
    token_rank = jnp.argsort(shuffles, axis=1).reshape(blocks, EXPERTS, TOK_DEV)
    member = (token_rank < counts[:, :, None]).astype(jnp.int32)
    member = jnp.transpose(member, (0, 2, 1))
    position = jnp.cumsum(member, axis=2) - member
    count_slab = jnp.sum(member, axis=2)
    columns = jnp.arange(TOPK)
    expert_numbers = jnp.arange(EXPERTS)
    slab_pick = jnp.sum(member[:, :, None, :] * (position[:, :, None, :] == columns[None, None, :, None]) * expert_numbers[None, None, None, :], axis=3)
    outside_span = ALL_EXP - EXPERTS
    offset = jax.random.randint(subkeys[3], (blocks, TOK_DEV), 0, outside_span)
    stride = jax.random.randint(subkeys[4], (blocks, TOK_DEV), 1, outside_span // TOPK + 1)
    outside = EXPERTS + (offset[:, :, None] + (columns[None, None, :] - count_slab[:, :, None]) * stride[:, :, None]) % outside_span
    chosen = jnp.where(columns[None, None, :] < count_slab[:, :, None], slab_pick, outside)
    rotation = jax.random.randint(subkeys[5], (blocks, TOK_DEV, 1), 0, TOPK)
    chosen = jnp.take_along_axis(chosen, (columns[None, None, :] + rotation) % TOPK, axis=2)
    return chosen.reshape(TOKENS, TOPK).astype(jnp.int32)


def steps_of(rng, dims, cuts, low, top_value):
    factor_of = 1.0
    for dim, blocks in cuts:
        draws = jax.random.uniform(jax.random.fold_in(jax.random.fold_in(rng, 6), dim), (blocks,), jnp.float32, low / len(cuts), top_value / len(cuts))
        factor_of = factor_of * jnp.repeat(jnp.exp(draws), dims[dim] // blocks).reshape((-1,) + (1,) * (len(dims) - 1 - dim))
    return factor_of


def centred(rng, extent, width, reach, cuts=(), kind=jnp.bfloat16):
    entries = width * jax.random.normal(rng, extent, jnp.float32)
    if cuts:
        entries = entries * steps_of(rng, extent, cuts, -0.22, 0.18)
    return jnp.clip(entries, -reach, reach).astype(kind)


def setup_inputs(seed: int = 0) -> dict:
    key_of = jax.random.split(jax.random.key(seed), 8)
    tokens = centred(key_of[0], (TOKENS, D), 1.0, 6.0, ((0, 32),))
    cotangent = centred(key_of[1], (TOKENS, D), 0.1, 0.59765625, ((0, 32),))
    route_ids = draw_route_ids(jax.random.fold_in(key_of[7], 71), 0)
    gates = jnp.clip(0.099609375 + 0.9003906 * jax.random.uniform(key_of[3], (TOKENS, TOPK), jnp.float32) ** steps_of(key_of[3], (TOKENS, TOPK), ((0, 32),), -0.2, 0.2), 0.099609375, 1.0).astype(jnp.bfloat16)
    w_gate = centred(key_of[4], (SLABS, D, HDEV), D ** -0.5, 0.09375, ((0, 16), (2, 2)))
    w_up = centred(key_of[5], (SLABS, D, HDEV), D ** -0.5, 0.09375, ((0, 16), (2, 2)))
    w_down = centred(key_of[6], (SLABS, D, HDEV), HID ** -0.5, 0.125, ((0, 16), (2, 2)))
    return dict(tokens=tokens, cotangent=cotangent, route_ids=route_ids, gates=gates, w_gate=w_gate, w_up=w_up, w_down=w_down)


def reference(tokens, cotangent, route_ids, gates, w_gate, w_up, w_down):
    blocks = TOKENS // TOK_DEV
    route_count = TOK_DEV * TOPK
    slot_total = EXPERTS * CAP
    flat_ids = route_ids.reshape(blocks, route_count)
    expert_hits = (flat_ids[:, :, None] == jnp.arange(EXPERTS, dtype=jnp.int32)[None, None, :]).astype(jnp.int32)
    earlier = jnp.cumsum(expert_hits, axis=1) - expert_hits
    slot_rank = jnp.sum(earlier * expert_hits, axis=2)
    in_slab = jnp.sum(expert_hits, axis=2) > 0
    slot_index = flat_ids * CAP + slot_rank
    table = (slot_index[:, :, None] == jnp.arange(slot_total, dtype=jnp.int32)[None, None, :]) & in_slab[:, :, None]
    route_token = jnp.arange(route_count, dtype=jnp.int32) // TOPK
    slot_token = jnp.sum(jnp.where(table, route_token[None, :, None], 0), axis=1).astype(jnp.int32)
    slot_live = jnp.any(table, axis=1)
    global_token = (slot_token + (jnp.arange(blocks, dtype=jnp.int32) * TOK_DEV)[:, None]).astype(jnp.int32)
    gate_flat = gates.reshape(blocks, route_count)[:, :, None].astype(jnp.float32)
    gate_slots = jnp.sum(jnp.where(table, gate_flat, 0.0), axis=1).astype(jnp.bfloat16)
    token_slots = jnp.where(slot_live[:, :, None], tokens[global_token], jnp.zeros((), tokens.dtype))
    cotan_slots = jnp.where(slot_live[:, :, None], cotangent[global_token], jnp.zeros((), cotangent.dtype))

    def by_expert(values):
        shaped = values.reshape((blocks, EXPERTS, CAP) + values.shape[2:])
        moved = jnp.moveaxis(shaped, 1, 0)
        return moved.reshape((EXPERTS, N_DP, SLABS * CAP) + values.shape[2:])

    expert_tokens = by_expert(token_slots)
    expert_cotan = by_expert(cotan_slots)
    expert_gates = by_expert(gate_slots)

    def dp_partial(left, right):
        summed = jnp.einsum("ird,irh->idh", left.astype(jnp.float32), right.astype(jnp.float32))
        rounded = lax.optimization_barrier(summed.astype(jnp.bfloat16))
        return jnp.sum(rounded.astype(jnp.float32), axis=0)

    def expert_work(operands):
        index, x_three, dy_three, g_two = operands
        slot_x = x_three.reshape(-1, D)
        slot_dy = dy_three.reshape(-1, D)
        slot_g = g_two.reshape(-1).astype(jnp.float32)[:, None]
        part_total = jnp.zeros((slot_x.shape[0], D), jnp.float32)
        score_total = jnp.zeros((slot_x.shape[0],), jnp.float32)
        grads_gate, grads_up, grads_down = [], [], []
        for block in range(HSPLIT):
            slab = index * HSPLIT + block
            gate_w = lax.dynamic_index_in_dim(w_gate, slab, 0, keepdims=False)
            up_w = lax.dynamic_index_in_dim(w_up, slab, 0, keepdims=False)
            down_w = lax.dynamic_index_in_dim(w_down, slab, 0, keepdims=False)
            pre_gate = jnp.dot(slot_x, gate_w, preferred_element_type=jnp.float32)
            pre_up = jnp.dot(slot_x, up_w, preferred_element_type=jnp.float32)
            sigmoid_gate = jax.nn.sigmoid(pre_gate)
            activation = pre_gate * sigmoid_gate
            hidden = (activation * pre_up).astype(jnp.bfloat16)
            back_proj = jnp.dot(slot_dy, down_w, preferred_element_type=jnp.float32)
            score_part = jnp.sum(hidden.astype(jnp.float32) * back_proj, axis=1).astype(jnp.bfloat16)
            scaled = slot_g * back_proj
            d_gate = (scaled * pre_up * sigmoid_gate * (1.0 + pre_gate * (1.0 - sigmoid_gate))).astype(jnp.bfloat16)
            d_up = (scaled * activation).astype(jnp.bfloat16)
            hidden_gated = (slot_g * hidden.astype(jnp.float32)).astype(jnp.bfloat16)
            partial_value = (jnp.dot(d_gate, gate_w.T, preferred_element_type=jnp.float32)
                       + jnp.dot(d_up, up_w.T, preferred_element_type=jnp.float32)).astype(jnp.bfloat16)
            part_total = part_total + partial_value.astype(jnp.float32)
            score_total = score_total + score_part.astype(jnp.float32)
            grads_gate.append(dp_partial(x_three, d_gate.reshape(N_DP, -1, HDEV)))
            grads_up.append(dp_partial(x_three, d_up.reshape(N_DP, -1, HDEV)))
            grads_down.append(dp_partial(dy_three, hidden_gated.reshape(N_DP, -1, HDEV)))
        return part_total, score_total, jnp.stack(grads_gate), jnp.stack(grads_up), jnp.stack(grads_down)

    parts, scores, grad_gate, grad_up, grad_down = lax.map(
        expert_work, (jnp.arange(EXPERTS, dtype=jnp.int32), expert_tokens, expert_cotan, expert_gates))
    grad_gate = grad_gate.reshape(SLABS, D, HDEV)
    grad_up = grad_up.reshape(SLABS, D, HDEV)
    grad_down = grad_down.reshape(SLABS, D, HDEV)
    parts_blocks = jnp.moveaxis(parts.reshape(EXPERTS, blocks, CAP, D), 0, 1).reshape(blocks, slot_total, D)
    scores_blocks = jnp.moveaxis(scores.reshape(EXPERTS, blocks, CAP), 0, 1).reshape(blocks, slot_total)
    live_parts = jnp.where(slot_live[:, :, None], parts_blocks, 0.0)
    token_grad = jnp.zeros((TOKENS, D), jnp.float32).at[global_token.reshape(-1)].add(live_parts.reshape(-1, D))
    gate_grad = jnp.einsum("brc,bc->br", table.astype(jnp.float32), scores_blocks, precision=lax.Precision.HIGHEST)
    return (w_gate, w_up, w_down, grad_gate, grad_up, grad_down,
            token_grad.astype(jnp.bfloat16), gate_grad.reshape(TOKENS, TOPK))
```

```python
import jax
import jax.numpy as jnp
from jax import lax
from jax.sharding import PartitionSpec as P

HSPLIT = 16
CAP = 6


def shards(tokens, cotangent, route_ids, gates, w_gate, w_up, w_down):
    slabs = lax.axis_size("expert")
    groups = lax.axis_size("dp")
    experts = slabs // HSPLIT
    tok_count, features = tokens.shape
    part = features // groups
    top_count = route_ids.shape[1]
    slot_total = experts * CAP
    flat_ids = route_ids.reshape(-1)
    expert_hits = (flat_ids[:, None] == jnp.arange(experts, dtype=jnp.int32)[None, :]).astype(
        jnp.int32
    )
    earlier = jnp.cumsum(expert_hits, axis=0) - expert_hits
    slot_rank = jnp.sum(earlier * expert_hits, axis=1)
    in_slab = jnp.sum(expert_hits, axis=1) > 0
    slot_index = flat_ids * CAP + slot_rank
    table = (slot_index[:, None] == jnp.arange(slot_total, dtype=jnp.int32)[None, :]) & in_slab[
        :, None
    ]
    select = table.reshape(tok_count, top_count, slot_total)
    picked = jnp.any(select, axis=1)
    pick_half = picked.astype(jnp.bfloat16)
    token_slots = jnp.einsum(
        "tc,td->cd", pick_half, tokens, preferred_element_type=jnp.float32
    ).astype(jnp.bfloat16)
    cotan_slots = jnp.einsum(
        "tc,td->cd", pick_half, cotangent, preferred_element_type=jnp.float32
    ).astype(jnp.bfloat16)
    gate_slots = jnp.sum(
        jnp.where(select, gates[:, :, None].astype(jnp.float32), 0.0), axis=(0, 1)
    ).astype(jnp.bfloat16)
    weights = jnp.stack([w_gate[0], w_up[0], w_down[0]])
    relaid = lax.all_to_all(weights, "dp", split_axis=1, concat_axis=2, tiled=True)
    both = jnp.stack([token_slots, cotan_slots]).reshape(2, experts, CAP, groups, part)
    both = jnp.moveaxis(both, 3, 0)
    both = lax.all_to_all(both, "dp", split_axis=0, concat_axis=0, tiled=True)
    gate_all = lax.all_gather(gate_slots.reshape(experts, CAP), "dp", axis=0, tiled=False)
    if experts == 1:
        recv = lax.all_gather(both, "expert", axis=0, tiled=False)[:, :, :, 0]
        gate_recv = lax.all_gather(gate_all, "expert", axis=0, tiled=False)[:, :, 0]
    else:
        send = jnp.repeat(jnp.moveaxis(both, 2, 0), HSPLIT, axis=0)
        recv = lax.all_to_all(send, "expert", split_axis=0, concat_axis=0, tiled=True)
        gate_send = jnp.repeat(jnp.moveaxis(gate_all, 1, 0), HSPLIT, axis=0)
        gate_recv = lax.all_to_all(gate_send, "expert", split_axis=0, concat_axis=0, tiled=True)
    slot_tokens = recv[:, :, 0].reshape(-1, part)
    slot_cotan = recv[:, :, 1].reshape(-1, part)
    slot_gates = gate_recv.reshape(-1).astype(jnp.float32)[:, None]
    pre_part = jnp.stack(
        [
            jnp.dot(slot_tokens, relaid[0], preferred_element_type=jnp.float32),
            jnp.dot(slot_tokens, relaid[1], preferred_element_type=jnp.float32),
            jnp.dot(slot_cotan, relaid[2], preferred_element_type=jnp.float32),
        ]
    )
    pre_gate, pre_up, back_proj = lax.psum(pre_part, "dp")
    sigmoid_gate = jax.nn.sigmoid(pre_gate)
    activation = pre_gate * sigmoid_gate
    hidden = (activation * pre_up).astype(jnp.bfloat16)
    score_part = jnp.sum(hidden.astype(jnp.float32) * back_proj, axis=1).astype(jnp.bfloat16)
    scaled = slot_gates * back_proj
    d_gate = (scaled * pre_up * sigmoid_gate * (1.0 + pre_gate * (1.0 - sigmoid_gate))).astype(
        jnp.bfloat16
    )
    d_up = (scaled * activation).astype(jnp.bfloat16)
    hidden_gated = (slot_gates * hidden.astype(jnp.float32)).astype(jnp.bfloat16)
    partial_value = (
        jnp.einsum("rh,dh->rd", d_gate, relaid[0], preferred_element_type=jnp.float32)
        + jnp.einsum("rh,dh->rd", d_up, relaid[1], preferred_element_type=jnp.float32)
    ).astype(jnp.bfloat16)
    grad_gate = jnp.einsum("rd,rh->dh", slot_tokens, d_gate, preferred_element_type=jnp.float32)
    grad_up = jnp.einsum("rd,rh->dh", slot_tokens, d_up, preferred_element_type=jnp.float32)
    grad_down = jnp.einsum(
        "rd,rh->dh", slot_cotan, hidden_gated, preferred_element_type=jnp.float32
    )
    rows = groups * CAP
    back_parts = lax.all_to_all(
        partial_value.reshape(slabs, rows, part), "expert", split_axis=0, concat_axis=0, tiled=True
    )
    back_scores = lax.all_to_all(
        score_part.reshape(slabs, rows), "expert", split_axis=0, concat_axis=0, tiled=True
    )
    part_sum = jnp.sum(
        back_parts.reshape(experts, HSPLIT, groups, CAP, part).astype(jnp.float32), axis=1
    ).astype(jnp.bfloat16)
    part_sum = lax.all_to_all(
        jnp.moveaxis(part_sum, 1, 0), "dp", split_axis=0, concat_axis=3, tiled=True
    ).reshape(slot_total, features)
    own = lax.axis_index("dp")
    score_sum = jnp.sum(
        back_scores.reshape(experts, HSPLIT, groups, CAP).astype(jnp.float32), axis=1
    )
    score_sum = lax.dynamic_index_in_dim(score_sum, own, 1, keepdims=False).reshape(slot_total)
    token_grad = jnp.einsum(
        "tc,cd->td", pick_half, part_sum, preferred_element_type=jnp.float32
    ).astype(jnp.bfloat16)
    gate_grad = jnp.einsum(
        "tkc,c->tk", select.astype(jnp.float32), score_sum, precision=lax.Precision.HIGHEST
    )
    return (
        relaid[0:1],
        relaid[1:2],
        relaid[2:3],
        grad_gate[None],
        grad_up[None],
        grad_down[None],
        token_grad,
        gate_grad,
    )


def solution(mesh):
    in_specs = (
        P(("dp", "expert"), None),
        P(("dp", "expert"), None),
        P(("dp", "expert"), None),
        P(("dp", "expert"), None),
        P("expert", None, "dp"),
        P("expert", None, "dp"),
        P("expert", None, "dp"),
    )
    out_specs = (
        P("expert", "dp", None),
        P("expert", "dp", None),
        P("expert", "dp", None),
        P("expert", "dp", None),
        P("expert", "dp", None),
        P("expert", "dp", None),
        P(("dp", "expert"), None),
        P(("dp", "expert"), None),
    )
    return jax.shard_map(shards, mesh=mesh, in_specs=in_specs, out_specs=out_specs, check_vma=False)
```

```python
import jax
import jax.numpy as jnp
from jax import lax
from jax.experimental import pallas as pl
from jax.experimental.pallas import tpu as pltpu
from jax.sharding import PartitionSpec as P

HSPLIT = 16
CAP = 6


MESH_ID = pl.DeviceIdType.MESH
LANES = 128
CHIPS = 8
Y_SLOTS, Y_GATE, Y_UP, Y_DOWN, Y_PRE, Y_SUM = range(6)
Z0, X0, C0, SIB, RET0, COPIES = 5, 9, 13, 21, 21, 29


def dot(left, right, left_dim, right_dim):
    return lax.dot_general(
        left, right, (((left_dim,), (right_dim,)), ((), ())), preferred_element_type=jnp.float32
    )


def exchange_kernel(
    tok_ref,
    cot_ref,
    ids_ref,
    gates_ref,
    wg_ref,
    wu_ref,
    wd_ref,
    relaid_gate_ref,
    relaid_up_ref,
    relaid_down_ref,
    grad_gate_ref,
    grad_up_ref,
    grad_down_ref,
    token_grad_ref,
    gate_grad_ref,
    slot_send,
    slot_recv,
    blocks,
    w2,
    w3,
    pre_send,
    pre_recv,
    hid,
    parts,
    sib_parts,
    chip_parts,
    final_parts,
    sum_send,
    sum_recv,
    send_sems,
    recv_sems,
):
    dp = lax.axis_index("dp")
    me = lax.axis_index("expert")
    half = w2.shape[1]
    wide = half + LANES
    core, chip = lax.rem(me, 2), lax.div(me, 2)
    side, lane = lax.rem(chip, 2), lax.div(chip, 2)

    def member(zz, xx, cc):
        return (zz * 2 + xx) * 2 + cc

    def z_at(step):
        return lax.rem(lane + step + 4, 4)

    partner = (1 - dp, me)
    sibling = (dp, member(lane, side, 1 - core))
    x_other = (dp, member(lane, 1 - side, core))

    def chip_at(step):
        return (dp, lax.rem(chip + step, CHIPS) * 2 + core)

    barrier = pltpu.get_barrier_semaphore()
    for other in [partner, sibling] + [chip_at(k) for k in range(1, CHIPS)]:
        pl.semaphore_signal(barrier, inc=1, device_id=other, device_id_type=MESH_ID)

    def copy(src, dst, number, device):
        out = pltpu.make_async_remote_copy(
            src_ref=src,
            dst_ref=dst,
            send_sem=send_sems.at[number],
            recv_sem=recv_sems.at[number],
            device_id=device,
            device_id_type=MESH_ID,
        )
        return out

    tok_count = ids_ref.shape[1]
    hits = (ids_ref[...] == 0).astype(jnp.float32)
    hit = jnp.sum(hits, axis=0, keepdims=True)
    earlier = (
        lax.broadcasted_iota(jnp.int32, (tok_count, tok_count), 0)
        < lax.broadcasted_iota(jnp.int32, (tok_count, tok_count), 1)
    ).astype(jnp.bfloat16)
    rank = dot(jnp.broadcast_to(hit, (16, tok_count)).astype(jnp.bfloat16), earlier, 1, 0)
    row = lax.broadcasted_iota(jnp.int32, (16, tok_count), 0)
    slot = rank.astype(jnp.int32)
    named = jnp.broadcast_to(hit, (16, tok_count))

    def placed(first):
        return jnp.where(row == slot + first, named, 0.0)

    pick = placed(0)
    gate_of = jnp.sum(hits * gates_ref[...].astype(jnp.float32), axis=0, keepdims=True)
    slot_gate = jnp.sum(pick * gate_of, axis=1, keepdims=True)
    pick_tok = pick.astype(jnp.bfloat16)
    pick_cot = placed(8).astype(jnp.bfloat16)

    def slots_of(which):
        cols = pl.ds(pl.multiple_of(which * half, LANES), half)
        return dot(pick_tok, tok_ref[:, cols], 1, 0) + dot(pick_cot, cot_ref[:, cols], 1, 0)

    gate_lanes = jnp.broadcast_to(slot_gate, (16, LANES))
    slot_send[:, :half] = slots_of(1 - dp).astype(jnp.bfloat16)
    slot_send[:, half:] = gate_lanes.astype(jnp.bfloat16)

    pl.semaphore_wait(barrier, CHIPS + 1)
    y_slots = copy(slot_send, slot_recv, Y_SLOTS, partner)
    y_slots.start()
    other_cols = pl.ds(pl.multiple_of((1 - dp) * half, LANES), half)
    own_cols = pl.ds(pl.multiple_of(dp * half, LANES), half)
    units = wg_ref.shape[0]
    rows_g = pl.ds(pl.multiple_of(dp * units, 64), units)
    rows_u = pl.ds(pl.multiple_of(2 * units + dp * units, 64), units)
    y_gate = copy(wg_ref.at[:, other_cols], w2.at[rows_g, :], Y_GATE, partner)
    y_up = copy(wu_ref.at[:, other_cols], w2.at[rows_u, :], Y_UP, partner)
    y_down = copy(wd_ref.at[:, other_cols], w3.at[rows_g, :], Y_DOWN, partner)
    y_gate.start()
    y_up.start()
    y_down.start()

    own = slots_of(dp)
    own = jnp.concatenate([own, gate_lanes], axis=1)
    w2[rows_g, :] = wg_ref[:, own_cols]
    w2[rows_u, :] = wu_ref[:, own_cols]
    w3[rows_g, :] = wd_ref[:, own_cols]
    y_slots.wait_recv()
    got = slot_recv[...].astype(jnp.float32)
    low = jnp.where(dp == 0, own, got)
    high = jnp.where(dp == 0, got, own)
    blocks[me, 0:16, :] = jnp.concatenate([low[0:8], high[0:8]], axis=0).astype(jnp.bfloat16)
    blocks[me, 16:32, :] = jnp.concatenate([low[8:16], high[8:16]], axis=0).astype(jnp.bfloat16)

    def send_block(source, number, device):
        out = copy(blocks.at[source], blocks.at[source], number, device)
        out.start()
        return out

    gathered = []
    along_z = [send_block(me, Z0 + k, (dp, member(z_at(k), side, core))) for k in range(1, 4)]
    along_x = [send_block(me, X0, x_other)]
    on_chip = [send_block(me, C0, sibling)]
    for k in range(1, 4):
        along_z[k - 1].wait_recv()
        source = member(z_at(-k), side, core)
        along_x.append(send_block(source, X0 + k, x_other))
        on_chip.append(send_block(source, C0 + 2 * k, sibling))
    for k in range(4):
        along_x[k].wait_recv()
        source = member(z_at(-k), 1 - side, core)
        on_chip.append(send_block(source, C0 + 2 * k + 1, sibling))
    for out in on_chip:
        out.wait_recv()
    gathered = along_z + along_x + on_chip

    total = blocks.shape[0] * 16
    slot_tok = blocks[:, 0:16, 0:half].reshape(total, half)
    slot_cot = blocks[:, 16:32, 0:half].reshape(total, half)
    slot_gates = blocks[:, 0:16, half:wide].reshape(total, LANES).astype(jnp.float32)
    y_gate.wait_recv()
    y_up.wait_recv()
    pre = dot(slot_tok, w2[...], 1, 1)
    pre_send[:, 0 : 2 * LANES] = pre.astype(jnp.bfloat16)
    y_down.wait_recv()
    back = dot(slot_cot, w3[...], 1, 1)
    pre_send[:, 2 * LANES :] = back.astype(jnp.bfloat16)
    y_pre = copy(pre_send, pre_recv, Y_PRE, partner)
    y_pre.start()
    relaid_gate_ref[...] = jnp.transpose(w2[0:LANES, :])
    relaid_up_ref[...] = jnp.transpose(w2[LANES:, :])
    relaid_down_ref[...] = jnp.transpose(w3[...])
    y_pre.wait_recv()
    pre_gate = pre[:, :LANES] + pre_recv[:, :LANES].astype(jnp.float32)
    pre_up = pre[:, LANES:] + pre_recv[:, LANES : 2 * LANES].astype(jnp.float32)
    back_proj = back + pre_recv[:, 2 * LANES :].astype(jnp.float32)
    sig = jax.nn.sigmoid(pre_gate)
    activation = pre_gate * sig
    hidden = (activation * pre_up).astype(jnp.bfloat16).astype(jnp.float32)
    score = jnp.sum(hidden * back_proj, axis=1, keepdims=True)
    scaled = slot_gates * back_proj
    hid[:, :LANES] = (scaled * pre_up * sig * (1.0 + pre_gate * (1.0 - sig))).astype(jnp.bfloat16)
    hid[:, LANES : 2 * LANES] = (scaled * activation).astype(jnp.bfloat16)
    hid[:, 2 * LANES :] = (slot_gates * hidden).astype(jnp.bfloat16)

    def put_parts(value, cols):
        split = value.astype(jnp.bfloat16).reshape(CHIPS, 2, 16, value.shape[1])
        parts[0, :, :, cols] = split[:, 0]
        parts[1, :, :, cols] = split[:, 1]

    put_parts(jnp.broadcast_to(score, (total, LANES)), pl.ds(half, LANES))
    d_both = hid[:, : 2 * LANES]
    for tile in range(half // 256):
        cols = pl.ds(tile * 256, 256)
        put_parts(dot(d_both, w2[:, cols], 1, 0), cols)
    to_sibling = copy(parts.at[1 - core], sib_parts, SIB, sibling)
    to_sibling.start()

    def grads(first, last):
        @pl.loop(first, last)
        def _(tile):
            cols = pl.ds(pl.multiple_of(tile * 256, 256), 256)
            x_tile = blocks[:, 0:16, cols].reshape(total, 256)
            y_tile = blocks[:, 16:32, cols].reshape(total, 256)
            both = dot(x_tile, hid[:, : 2 * LANES], 0, 0)
            grad_gate_ref[cols, :] = both[:, :LANES]
            grad_up_ref[cols, :] = both[:, LANES:]
            grad_down_ref[cols, :] = dot(y_tile, hid[:, 2 * LANES :], 0, 0)

    grads(0, 1)
    to_sibling.wait_recv()
    returned = []
    for k in range(CHIPS):
        dest = lax.rem(chip + k, CHIPS)
        both = parts[core, dest].astype(jnp.float32) + sib_parts[dest].astype(jnp.float32)
        if k == 0:
            own_sum = both
        else:
            chip_parts[k] = both.astype(jnp.bfloat16)
            out = copy(chip_parts.at[k], final_parts.at[k], RET0 + k, chip_at(k))
            out.start()
            returned.append(out)
    grads(1, half // 256)
    for k in range(1, CHIPS):
        returned[k - 1].wait_recv()
        own_sum = own_sum + final_parts[k].astype(jnp.float32)
    sum_send[...] = own_sum[:, :half].astype(jnp.bfloat16)
    y_sum = copy(sum_send, sum_recv, Y_SUM, partner)
    y_sum.start()
    pick_mine = placed(8 * dp)
    score_of = jnp.sum(pick_mine * own_sum[:, half:], axis=0, keepdims=True)
    gate_grad_ref[...] = hits * score_of
    pick_half = pick_mine.astype(jnp.bfloat16)
    token_grad_ref[:, own_cols] = dot(pick_half, sum_send[...], 0, 0).astype(jnp.bfloat16)
    y_sum.wait_recv()
    token_grad_ref[:, other_cols] = dot(pick_half, sum_recv[...], 0, 0).astype(jnp.bfloat16)
    for out in [y_slots, y_gate, y_up, y_down, y_pre, y_sum, to_sibling] + gathered + returned:
        out.wait_send()


def one_expert(tokens, cotangent, route_ids, gates, w_gate, w_up, w_down):
    slabs = lax.axis_size("expert")
    tok_count, features = tokens.shape
    top_count = route_ids.shape[1]
    half = features // 2
    wide = half + LANES
    total = slabs * 16
    bf16, f32 = jnp.bfloat16, jnp.float32
    vmem = pl.BlockSpec(memory_space=pltpu.VMEM)
    outs = pl.pallas_call(
        exchange_kernel,
        out_shape=[jax.ShapeDtypeStruct((half, LANES), bf16)] * 3
        + [jax.ShapeDtypeStruct((half, LANES), f32)] * 3
        + [
            jax.ShapeDtypeStruct((tok_count, features), bf16),
            jax.ShapeDtypeStruct((top_count, tok_count), f32),
        ],
        in_specs=[vmem] * 7,
        out_specs=[vmem] * 8,
        scratch_shapes=[
            pltpu.VMEM((16, wide), bf16),
            pltpu.VMEM((16, wide), bf16),
            pltpu.VMEM((slabs, 32, wide), bf16),
            pltpu.VMEM((2 * LANES, half), bf16),
            pltpu.VMEM((LANES, half), bf16),
            pltpu.VMEM((total, 3 * LANES), bf16),
            pltpu.VMEM((total, 3 * LANES), bf16),
            pltpu.VMEM((total, 3 * LANES), bf16),
            pltpu.VMEM((2, CHIPS, 16, wide), bf16),
            pltpu.VMEM((CHIPS, 16, wide), bf16),
            pltpu.VMEM((CHIPS, 16, wide), bf16),
            pltpu.VMEM((CHIPS, 16, wide), bf16),
            pltpu.VMEM((16, half), bf16),
            pltpu.VMEM((16, half), bf16),
            pltpu.SemaphoreType.DMA((COPIES,)),
            pltpu.SemaphoreType.DMA((COPIES,)),
        ],
        compiler_params=pltpu.CompilerParams(
            collective_id=0, has_side_effects=True, vmem_limit_bytes=48 * 2**20
        ),
        cost_estimate=pl.CostEstimate(
            flops=16 * total * half * LANES, bytes_accessed=12 * 2**20, transcendentals=total * LANES
        ),
    )(
        tokens,
        cotangent,
        route_ids.T,
        gates.T,
        w_gate[0].T,
        w_up[0].T,
        w_down[0].T,
    )
    return tuple(value[None] for value in outs[:6]) + (outs[6], outs[7].T)


def shards(tokens, cotangent, route_ids, gates, w_gate, w_up, w_down):
    slabs = lax.axis_size("expert")
    groups = lax.axis_size("dp")
    experts = slabs // HSPLIT
    tok_count, features = tokens.shape
    part = features // groups
    top_count = route_ids.shape[1]
    slot_total = experts * CAP
    flat_ids = route_ids.reshape(-1)
    expert_hits = (flat_ids[:, None] == jnp.arange(experts, dtype=jnp.int32)[None, :]).astype(
        jnp.int32
    )
    earlier = jnp.cumsum(expert_hits, axis=0) - expert_hits
    slot_rank = jnp.sum(earlier * expert_hits, axis=1)
    in_slab = jnp.sum(expert_hits, axis=1) > 0
    slot_index = flat_ids * CAP + slot_rank
    table = (slot_index[:, None] == jnp.arange(slot_total, dtype=jnp.int32)[None, :]) & in_slab[
        :, None
    ]
    select = table.reshape(tok_count, top_count, slot_total)
    picked = jnp.any(select, axis=1)
    pick_half = picked.astype(jnp.bfloat16)
    token_slots = jnp.einsum(
        "tc,td->cd", pick_half, tokens, preferred_element_type=jnp.float32
    ).astype(jnp.bfloat16)
    cotan_slots = jnp.einsum(
        "tc,td->cd", pick_half, cotangent, preferred_element_type=jnp.float32
    ).astype(jnp.bfloat16)
    gate_slots = jnp.sum(
        jnp.where(select, gates[:, :, None].astype(jnp.float32), 0.0), axis=(0, 1)
    ).astype(jnp.bfloat16)
    weights = jnp.stack([w_gate[0], w_up[0], w_down[0]])
    relaid = lax.all_to_all(weights, "dp", split_axis=1, concat_axis=2, tiled=True)
    both = jnp.stack([token_slots, cotan_slots]).reshape(2, experts, CAP, groups, part)
    both = jnp.moveaxis(both, 3, 0)
    both = lax.all_to_all(both, "dp", split_axis=0, concat_axis=0, tiled=True)
    gate_all = lax.all_gather(gate_slots.reshape(experts, CAP), "dp", axis=0, tiled=False)
    if experts == 1:
        recv = lax.all_gather(both, "expert", axis=0, tiled=False)[:, :, :, 0]
        gate_recv = lax.all_gather(gate_all, "expert", axis=0, tiled=False)[:, :, 0]
    else:
        send = jnp.repeat(jnp.moveaxis(both, 2, 0), HSPLIT, axis=0)
        recv = lax.all_to_all(send, "expert", split_axis=0, concat_axis=0, tiled=True)
        gate_send = jnp.repeat(jnp.moveaxis(gate_all, 1, 0), HSPLIT, axis=0)
        gate_recv = lax.all_to_all(gate_send, "expert", split_axis=0, concat_axis=0, tiled=True)
    slot_tokens = recv[:, :, 0].reshape(-1, part)
    slot_cotan = recv[:, :, 1].reshape(-1, part)
    slot_gates = gate_recv.reshape(-1).astype(jnp.float32)[:, None]
    pre_part = jnp.stack(
        [
            jnp.dot(slot_tokens, relaid[0], preferred_element_type=jnp.float32),
            jnp.dot(slot_tokens, relaid[1], preferred_element_type=jnp.float32),
            jnp.dot(slot_cotan, relaid[2], preferred_element_type=jnp.float32),
        ]
    )
    pre_gate, pre_up, back_proj = lax.psum(pre_part, "dp")
    sigmoid_gate = jax.nn.sigmoid(pre_gate)
    activation = pre_gate * sigmoid_gate
    hidden = (activation * pre_up).astype(jnp.bfloat16)
    score_part = jnp.sum(hidden.astype(jnp.float32) * back_proj, axis=1).astype(jnp.bfloat16)
    scaled = slot_gates * back_proj
    d_gate = (scaled * pre_up * sigmoid_gate * (1.0 + pre_gate * (1.0 - sigmoid_gate))).astype(
        jnp.bfloat16
    )
    d_up = (scaled * activation).astype(jnp.bfloat16)
    hidden_gated = (slot_gates * hidden.astype(jnp.float32)).astype(jnp.bfloat16)
    partial_value = (
        jnp.einsum("rh,dh->rd", d_gate, relaid[0], preferred_element_type=jnp.float32)
        + jnp.einsum("rh,dh->rd", d_up, relaid[1], preferred_element_type=jnp.float32)
    ).astype(jnp.bfloat16)
    grad_gate = jnp.einsum("rd,rh->dh", slot_tokens, d_gate, preferred_element_type=jnp.float32)
    grad_up = jnp.einsum("rd,rh->dh", slot_tokens, d_up, preferred_element_type=jnp.float32)
    grad_down = jnp.einsum(
        "rd,rh->dh", slot_cotan, hidden_gated, preferred_element_type=jnp.float32
    )
    rows = groups * CAP
    back_parts = lax.all_to_all(
        partial_value.reshape(slabs, rows, part), "expert", split_axis=0, concat_axis=0, tiled=True
    )
    back_scores = lax.all_to_all(
        score_part.reshape(slabs, rows), "expert", split_axis=0, concat_axis=0, tiled=True
    )
    part_sum = jnp.sum(
        back_parts.reshape(experts, HSPLIT, groups, CAP, part).astype(jnp.float32), axis=1
    ).astype(jnp.bfloat16)
    part_sum = lax.all_to_all(
        jnp.moveaxis(part_sum, 1, 0), "dp", split_axis=0, concat_axis=3, tiled=True
    ).reshape(slot_total, features)
    own = lax.axis_index("dp")
    score_sum = jnp.sum(
        back_scores.reshape(experts, HSPLIT, groups, CAP).astype(jnp.float32), axis=1
    )
    score_sum = lax.dynamic_index_in_dim(score_sum, own, 1, keepdims=False).reshape(slot_total)
    token_grad = jnp.einsum(
        "tc,cd->td", pick_half, part_sum, preferred_element_type=jnp.float32
    ).astype(jnp.bfloat16)
    gate_grad = jnp.einsum(
        "tkc,c->tk", select.astype(jnp.float32), score_sum, precision=lax.Precision.HIGHEST
    )
    return (
        relaid[0:1],
        relaid[1:2],
        relaid[2:3],
        grad_gate[None],
        grad_up[None],
        grad_down[None],
        token_grad,
        gate_grad,
    )


def solution(mesh):
    in_specs = (
        P(("dp", "expert"), None),
        P(("dp", "expert"), None),
        P(("dp", "expert"), None),
        P(("dp", "expert"), None),
        P("expert", None, "dp"),
        P("expert", None, "dp"),
        P("expert", None, "dp"),
    )
    out_specs = (
        P("expert", "dp", None),
        P("expert", "dp", None),
        P("expert", "dp", None),
        P("expert", "dp", None),
        P("expert", "dp", None),
        P("expert", "dp", None),
        P(("dp", "expert"), None),
        P(("dp", "expert"), None),
    )
    fits = mesh.shape["dp"] == 2 and mesh.shape["expert"] == HSPLIT
    body = one_expert if fits else shards
    return jax.shard_map(body, mesh=mesh, in_specs=in_specs, out_specs=out_specs, check_vma=False)
```

```python
import jax
import jax.numpy as jnp
from jax import lax
from jax.experimental import pallas as pl
from jax.experimental.pallas import tpu as pltpu
from jax.sharding import PartitionSpec as P

HSPLIT = 16
CAP = 6


MESH_ID = pl.DeviceIdType.MESH
LANES = 128
CHIPS = 8
Y_SLOTS, Y_GATE, Y_UP, Y_DOWN, Y_PRE, Y_SUM, Y_BACK = range(7)
Z0, X0, C0, SIB, RX0, RZ0, COPIES = 6, 10, 14, 22, 23, 26, 30


def dot(left, right, left_dim, right_dim):
    return lax.dot_general(
        left, right, (((left_dim,), (right_dim,)), ((), ())), preferred_element_type=jnp.float32
    )


def exchange_kernel(
    tok_ref,
    cot_ref,
    ids_ref,
    gates_ref,
    wg_ref,
    wu_ref,
    wd_ref,
    relaid_gate_out,
    relaid_up_out,
    relaid_down_out,
    grad_gate_out,
    grad_up_out,
    grad_down_out,
    token_grad_out,
    gate_grad_ref,
    slot_send,
    slot_recv,
    blocks,
    w2,
    w3,
    pre_send,
    pre_recv,
    hid,
    hid_core,
    parts,
    sib_parts,
    x_send,
    x_recv,
    z_send,
    z_recv,
    sum_send,
    sum_recv,
    tok_vmem,
    cot_vmem,
    relaid_gate_ref,
    relaid_up_ref,
    relaid_down_ref,
    grad_gate_ref,
    grad_up_ref,
    grad_down_ref,
    token_grad_ref,
    send_sems,
    recv_sems,
    local_sems,
):
    dp = lax.axis_index("dp")
    me = lax.axis_index("expert")
    half = w2.shape[1]
    wide = half + LANES
    core, chip = lax.rem(me, 2), lax.div(me, 2)
    side, lane = lax.rem(chip, 2), lax.div(chip, 2)

    def member(zz, xx, cc):
        return (zz * 2 + xx) * 2 + cc

    def z_at(step):
        return lax.rem(lane + step + 4, 4)

    partner = (1 - dp, me)
    sibling = (dp, member(lane, side, 1 - core))
    x_other = (dp, member(lane, 1 - side, core))

    def chip_at(step):
        return (dp, lax.rem(chip + step, CHIPS) * 2 + core)

    barrier = pltpu.get_barrier_semaphore()
    for other in [partner, sibling] + [chip_at(k) for k in range(1, CHIPS)]:
        pl.semaphore_signal(barrier, inc=1, device_id=other, device_id_type=MESH_ID)

    def copy(src, dst, number, device):
        out = pltpu.make_async_remote_copy(
            src_ref=src,
            dst_ref=dst,
            send_sem=send_sems.at[number],
            recv_sem=recv_sems.at[number],
            device_id=device,
            device_id_type=MESH_ID,
        )
        return out

    other_cols = pl.ds(pl.multiple_of((1 - dp) * half, LANES), half)
    own_cols = pl.ds(pl.multiple_of(dp * half, LANES), half)
    units = wg_ref.shape[0]
    rows_g = pl.ds(pl.multiple_of(dp * units, 64), units)
    rows_u = pl.ds(pl.multiple_of(2 * units + dp * units, 64), units)
    local = [
        pltpu.make_async_copy(source, target, local_sems.at[number])
        for number, (source, target) in enumerate(
            [
                (tok_ref, tok_vmem),
                (cot_ref, cot_vmem),
                (wg_ref.at[:, own_cols], w2.at[rows_g, :]),
                (wu_ref.at[:, own_cols], w2.at[rows_u, :]),
                (wd_ref.at[:, own_cols], w3.at[rows_g, :]),
            ]
        )
    ]
    for out in local:
        out.start()

    def store(number, source, target):
        out = pltpu.make_async_copy(source, target, local_sems.at[5 + number])
        out.start()
        return out

    tok_count = ids_ref.shape[1]
    hits = (ids_ref[...] == 0).astype(jnp.float32)
    hit = jnp.sum(hits, axis=0, keepdims=True)
    earlier = (
        lax.broadcasted_iota(jnp.int32, (tok_count, tok_count), 0)
        < lax.broadcasted_iota(jnp.int32, (tok_count, tok_count), 1)
    ).astype(jnp.bfloat16)
    rank = dot(jnp.broadcast_to(hit, (16, tok_count)).astype(jnp.bfloat16), earlier, 1, 0)
    row = lax.broadcasted_iota(jnp.int32, (16, tok_count), 0)
    slot = rank.astype(jnp.int32)
    named = jnp.broadcast_to(hit, (16, tok_count))

    def placed(first):
        return jnp.where(row == slot + first, named, 0.0)

    pick = placed(0)
    gate_of = jnp.sum(hits * gates_ref[...].astype(jnp.float32), axis=0, keepdims=True)
    slot_gate = jnp.sum(pick * gate_of, axis=1, keepdims=True)
    pick_tok = pick.astype(jnp.bfloat16)
    pick_cot = placed(8).astype(jnp.bfloat16)

    def slots_of(which):
        cols = pl.ds(pl.multiple_of(which * half, LANES), half)
        return dot(pick_tok, tok_vmem[:, cols], 1, 0) + dot(pick_cot, cot_vmem[:, cols], 1, 0)

    y_gate = copy(wg_ref.at[:, other_cols], w2.at[rows_g, :], Y_GATE, partner)
    y_up = copy(wu_ref.at[:, other_cols], w2.at[rows_u, :], Y_UP, partner)
    y_down = copy(wd_ref.at[:, other_cols], w3.at[rows_g, :], Y_DOWN, partner)
    pl.semaphore_wait(barrier, CHIPS + 1)
    y_gate.start()
    local[0].wait()
    local[1].wait()
    gate_lanes = jnp.broadcast_to(slot_gate, (16, LANES))
    slot_send[:, :half] = slots_of(1 - dp).astype(jnp.bfloat16)
    slot_send[:, half:] = gate_lanes.astype(jnp.bfloat16)
    y_slots = copy(slot_send, slot_recv, Y_SLOTS, partner)
    y_slots.start()
    y_up.start()
    y_down.start()

    own = slots_of(dp)
    own = jnp.concatenate([own, gate_lanes], axis=1)
    y_slots.wait_recv()
    got = slot_recv[...].astype(jnp.float32)
    low = jnp.where(dp == 0, own, got)
    high = jnp.where(dp == 0, got, own)
    blocks[me, 0:16, :] = jnp.concatenate([low[0:8], high[0:8]], axis=0).astype(jnp.bfloat16)
    blocks[me, 16:32, :] = jnp.concatenate([low[8:16], high[8:16]], axis=0).astype(jnp.bfloat16)

    def send_block(source, number, device):
        out = copy(blocks.at[source], blocks.at[source], number, device)
        out.start()
        return out

    gathered = []
    along_z = [send_block(me, Z0 + k, (dp, member(z_at(k), side, core))) for k in range(1, 4)]
    along_x = [send_block(me, X0, x_other)]
    on_chip = [send_block(me, C0, sibling)]
    for k in range(1, 4):
        along_z[k - 1].wait_recv()
        source = member(z_at(-k), side, core)
        along_x.append(send_block(source, X0 + k, x_other))
        on_chip.append(send_block(source, C0 + 2 * k, sibling))
    for k in range(4):
        along_x[k].wait_recv()
        source = member(z_at(-k), 1 - side, core)
        on_chip.append(send_block(source, C0 + 2 * k + 1, sibling))
    for out in on_chip:
        out.wait_recv()
    gathered = along_z + along_x + on_chip

    total = blocks.shape[0] * 16
    slot_tok = blocks[:, 0:16, 0:half].reshape(total, half)
    slot_cot = blocks[:, 16:32, 0:half].reshape(total, half)
    slot_gates = blocks[:, 0:16, half:wide].reshape(total, LANES).astype(jnp.float32)
    for out in local[2:]:
        out.wait()
    y_gate.wait_recv()
    y_up.wait_recv()
    pre = dot(slot_tok, w2[...], 1, 1)
    fore, aft = pl.ds(0, 2 * LANES), pl.ds(2 * LANES, LANES)
    pre_send[:, fore] = pre.astype(jnp.bfloat16)
    y_pre = copy(pre_send.at[:, fore], pre_recv.at[:, fore], Y_PRE, partner)
    y_pre.start()
    relaid_gate_ref[...] = jnp.transpose(w2[0:LANES, :])
    relaid_up_ref[...] = jnp.transpose(w2[LANES:, :])
    y_down.wait_recv()
    back = dot(slot_cot, w3[...], 1, 1)
    pre_send[:, aft] = back.astype(jnp.bfloat16)
    y_back = copy(pre_send.at[:, aft], pre_recv.at[:, aft], Y_BACK, partner)
    y_back.start()
    relaid_down_ref[...] = jnp.transpose(w3[...])
    stores = [
        store(0, relaid_gate_ref, relaid_gate_out),
        store(1, relaid_up_ref, relaid_up_out),
        store(2, relaid_down_ref, relaid_down_out),
    ]
    y_pre.wait_recv()
    y_back.wait_recv()
    pre_gate = pre[:, :LANES] + pre_recv[:, :LANES].astype(jnp.float32)
    pre_up = pre[:, LANES:] + pre_recv[:, LANES : 2 * LANES].astype(jnp.float32)
    back_proj = back + pre_recv[:, 2 * LANES :].astype(jnp.float32)
    sig = jax.nn.sigmoid(pre_gate)
    activation = pre_gate * sig
    hidden = (activation * pre_up).astype(jnp.bfloat16).astype(jnp.float32)
    score = jnp.sum(hidden * back_proj, axis=1, keepdims=True)
    scaled = slot_gates * back_proj
    d_gate = (scaled * pre_up * sig * (1.0 + pre_gate * (1.0 - sig))).astype(jnp.bfloat16)
    d_up = (scaled * activation).astype(jnp.bfloat16)
    by_core = jnp.concatenate([d_gate, d_up], axis=1)
    hid[:, : 2 * LANES] = by_core
    hid[:, 2 * LANES :] = (slot_gates * hidden).astype(jnp.bfloat16)
    by_core = by_core.reshape(CHIPS, 2, 16, 2 * LANES)
    hid_core[0] = by_core[:, 0].reshape(total // 2, 2 * LANES)
    hid_core[1] = by_core[:, 1].reshape(total // 2, 2 * LANES)
    scores = jnp.broadcast_to(score, (total, LANES)).astype(jnp.bfloat16)
    scores = scores.reshape(CHIPS, 2, 16, LANES)
    parts[0, :, :, half:] = scores[:, 0]
    parts[1, :, :, half:] = scores[:, 1]

    def put_parts(to):
        for tile in range(half // 256):
            cols = pl.ds(tile * 256, 256)
            value = dot(hid_core[to], w2[:, cols], 1, 0).astype(jnp.bfloat16)
            parts[to, :, :, cols] = value.reshape(CHIPS, 16, 256)

    put_parts(1 - core)
    to_sibling = copy(parts.at[1 - core], sib_parts, SIB, sibling)
    to_sibling.start()
    put_parts(core)

    def grads(first, last):
        @pl.loop(first, last)
        def _(tile):
            cols = pl.ds(pl.multiple_of(tile * 256, 256), 256)
            x_tile = blocks[:, 0:16, cols].reshape(total, 256)
            y_tile = blocks[:, 16:32, cols].reshape(total, 256)
            both = dot(x_tile, hid[:, : 2 * LANES], 0, 0)
            grad_gate_ref[cols, :] = both[:, :LANES]
            grad_up_ref[cols, :] = both[:, LANES:]
            grad_down_ref[cols, :] = dot(y_tile, hid[:, 2 * LANES :], 0, 0)

    grads(0, 1)
    to_sibling.wait_recv()
    def chip_sum(dest):
        return parts[core, dest].astype(jnp.float32) + sib_parts[dest].astype(jnp.float32)

    returned, across_x, back_z = [], {}, []
    order = (2, 1, 3, 0)
    for k in order:
        x_send[k] = chip_sum(z_at(k) * 2 + 1 - side).astype(jnp.bfloat16)
        across_x[k] = copy(x_send.at[k], x_recv.at[k], RX0 + k, x_other)
        across_x[k].start()
        returned.append(across_x[k])
    for k in order:
        across_x[k].wait_recv()
        own_sum = chip_sum(z_at(k) * 2 + side) + x_recv[k].astype(jnp.float32)
        if k:
            z_send[k] = own_sum.astype(jnp.bfloat16)
            out = copy(z_send.at[k], z_recv.at[k], RZ0 + k, (dp, member(z_at(k), side, core)))
            out.start()
            back_z.append((k, out))
            returned.append(out)
    grads(1, half // 256)
    stores += [
        store(3, grad_gate_ref, grad_gate_out),
        store(4, grad_up_ref, grad_up_out),
        store(5, grad_down_ref, grad_down_out),
    ]
    for k, out in back_z:
        out.wait_recv()
        own_sum = own_sum + z_recv[k].astype(jnp.float32)
    sum_send[...] = own_sum[:, :half].astype(jnp.bfloat16)
    y_sum = copy(sum_send, sum_recv, Y_SUM, partner)
    y_sum.start()
    pick_mine = placed(8 * dp)
    score_of = jnp.sum(pick_mine * own_sum[:, half:], axis=0, keepdims=True)
    gate_grad_ref[...] = hits * score_of
    pick_half = pick_mine.astype(jnp.bfloat16)
    token_grad_ref[:, own_cols] = dot(pick_half, sum_send[...], 0, 0).astype(jnp.bfloat16)
    y_sum.wait_recv()
    token_grad_ref[:, other_cols] = dot(pick_half, sum_recv[...], 0, 0).astype(jnp.bfloat16)
    stores.append(store(6, token_grad_ref, token_grad_out))
    for out in stores:
        out.wait()
    for out in [y_slots, y_gate, y_up, y_down, y_pre, y_back, y_sum, to_sibling] + gathered + returned:
        out.wait_send()


def store_kernel(*refs):
    sources, targets, sems = refs[:8], refs[8:16], refs[16]
    stores = [
        pltpu.make_async_copy(sources[i], targets[i], sems.at[i]) for i in range(8)
    ]
    for out in stores:
        out.start()
    for out in stores:
        out.wait()


def one_expert(tokens, cotangent, route_ids, gates, w_gate, w_up, w_down):
    slabs = lax.axis_size("expert")
    tok_count, features = tokens.shape
    top_count = route_ids.shape[1]
    half = features // 2
    wide = half + LANES
    total = slabs * 16
    bf16, f32 = jnp.bfloat16, jnp.float32
    vmem = pl.BlockSpec(memory_space=pltpu.VMEM)
    hbm = pl.BlockSpec(memory_space=pltpu.HBM)
    outs = pl.pallas_call(
        exchange_kernel,
        out_shape=[jax.ShapeDtypeStruct((half, LANES), bf16)] * 3
        + [jax.ShapeDtypeStruct((half, LANES), f32)] * 3
        + [
            jax.ShapeDtypeStruct((tok_count, features), bf16),
            jax.ShapeDtypeStruct((top_count, tok_count), f32),
        ],
        in_specs=[hbm, hbm, vmem, vmem, hbm, hbm, hbm],
        out_specs=[hbm] * 7 + [vmem],
        scratch_shapes=[
            pltpu.VMEM((16, wide), bf16),
            pltpu.VMEM((16, wide), bf16),
            pltpu.VMEM((slabs, 32, wide), bf16),
            pltpu.VMEM((2 * LANES, half), bf16),
            pltpu.VMEM((LANES, half), bf16),
            pltpu.VMEM((total, 3 * LANES), bf16),
            pltpu.VMEM((total, 3 * LANES), bf16),
            pltpu.VMEM((total, 3 * LANES), bf16),
            pltpu.VMEM((2, total // 2, 2 * LANES), bf16),
            pltpu.VMEM((2, CHIPS, 16, wide), bf16),
            pltpu.VMEM((CHIPS, 16, wide), bf16),
            pltpu.VMEM((4, 16, wide), bf16),
            pltpu.VMEM((4, 16, wide), bf16),
            pltpu.VMEM((4, 16, wide), bf16),
            pltpu.VMEM((4, 16, wide), bf16),
            pltpu.VMEM((16, half), bf16),
            pltpu.VMEM((16, half), bf16),
            pltpu.VMEM((tok_count, features), bf16),
            pltpu.VMEM((tok_count, features), bf16),
            pltpu.VMEM((half, LANES), bf16),
            pltpu.VMEM((half, LANES), bf16),
            pltpu.VMEM((half, LANES), bf16),
            pltpu.VMEM((half, LANES), f32),
            pltpu.VMEM((half, LANES), f32),
            pltpu.VMEM((half, LANES), f32),
            pltpu.VMEM((tok_count, features), bf16),
            pltpu.SemaphoreType.DMA((COPIES,)),
            pltpu.SemaphoreType.DMA((COPIES,)),
            pltpu.SemaphoreType.DMA((12,)),
        ],
        compiler_params=pltpu.CompilerParams(
            collective_id=0, has_side_effects=True, vmem_limit_bytes=58 * 2**20
        ),
        cost_estimate=pl.CostEstimate(
            flops=16 * total * half * LANES, bytes_accessed=12 * 2**20, transcendentals=total * LANES
        ),
    )(
        tokens,
        cotangent,
        route_ids.T,
        gates.T,
        w_gate[0].T,
        w_up[0].T,
        w_down[0].T,
    )
    outs = pl.pallas_call(
        store_kernel,
        out_shape=[jax.ShapeDtypeStruct(value.shape, value.dtype) for value in outs],
        in_specs=[hbm] * 8,
        out_specs=[hbm] * 8,
        scratch_shapes=[pltpu.SemaphoreType.DMA((8,))],
        compiler_params=pltpu.CompilerParams(vmem_limit_bytes=58 * 2**20),
        cost_estimate=pl.CostEstimate(flops=0, bytes_accessed=10 * 2**20, transcendentals=0),
    )(*outs)
    return tuple(value[None] for value in outs[:6]) + (outs[6], outs[7].T)


def shards(tokens, cotangent, route_ids, gates, w_gate, w_up, w_down):
    slabs = lax.axis_size("expert")
    groups = lax.axis_size("dp")
    experts = slabs // HSPLIT
    tok_count, features = tokens.shape
    part = features // groups
    top_count = route_ids.shape[1]
    slot_total = experts * CAP
    flat_ids = route_ids.reshape(-1)
    expert_hits = (flat_ids[:, None] == jnp.arange(experts, dtype=jnp.int32)[None, :]).astype(
        jnp.int32
    )
    earlier = jnp.cumsum(expert_hits, axis=0) - expert_hits
    slot_rank = jnp.sum(earlier * expert_hits, axis=1)
    in_slab = jnp.sum(expert_hits, axis=1) > 0
    slot_index = flat_ids * CAP + slot_rank
    table = (slot_index[:, None] == jnp.arange(slot_total, dtype=jnp.int32)[None, :]) & in_slab[
        :, None
    ]
    select = table.reshape(tok_count, top_count, slot_total)
    picked = jnp.any(select, axis=1)
    pick_half = picked.astype(jnp.bfloat16)
    token_slots = jnp.einsum(
        "tc,td->cd", pick_half, tokens, preferred_element_type=jnp.float32
    ).astype(jnp.bfloat16)
    cotan_slots = jnp.einsum(
        "tc,td->cd", pick_half, cotangent, preferred_element_type=jnp.float32
    ).astype(jnp.bfloat16)
    gate_slots = jnp.sum(
        jnp.where(select, gates[:, :, None].astype(jnp.float32), 0.0), axis=(0, 1)
    ).astype(jnp.bfloat16)
    weights = jnp.stack([w_gate[0], w_up[0], w_down[0]])
    relaid = lax.all_to_all(weights, "dp", split_axis=1, concat_axis=2, tiled=True)
    both = jnp.stack([token_slots, cotan_slots]).reshape(2, experts, CAP, groups, part)
    both = jnp.moveaxis(both, 3, 0)
    both = lax.all_to_all(both, "dp", split_axis=0, concat_axis=0, tiled=True)
    gate_all = lax.all_gather(gate_slots.reshape(experts, CAP), "dp", axis=0, tiled=False)
    if experts == 1:
        recv = lax.all_gather(both, "expert", axis=0, tiled=False)[:, :, :, 0]
        gate_recv = lax.all_gather(gate_all, "expert", axis=0, tiled=False)[:, :, 0]
    else:
        send = jnp.repeat(jnp.moveaxis(both, 2, 0), HSPLIT, axis=0)
        recv = lax.all_to_all(send, "expert", split_axis=0, concat_axis=0, tiled=True)
        gate_send = jnp.repeat(jnp.moveaxis(gate_all, 1, 0), HSPLIT, axis=0)
        gate_recv = lax.all_to_all(gate_send, "expert", split_axis=0, concat_axis=0, tiled=True)
    slot_tokens = recv[:, :, 0].reshape(-1, part)
    slot_cotan = recv[:, :, 1].reshape(-1, part)
    slot_gates = gate_recv.reshape(-1).astype(jnp.float32)[:, None]
    pre_part = jnp.stack(
        [
            jnp.dot(slot_tokens, relaid[0], preferred_element_type=jnp.float32),
            jnp.dot(slot_tokens, relaid[1], preferred_element_type=jnp.float32),
            jnp.dot(slot_cotan, relaid[2], preferred_element_type=jnp.float32),
        ]
    )
    pre_gate, pre_up, back_proj = lax.psum(pre_part, "dp")
    sigmoid_gate = jax.nn.sigmoid(pre_gate)
    activation = pre_gate * sigmoid_gate
    hidden = (activation * pre_up).astype(jnp.bfloat16)
    score_part = jnp.sum(hidden.astype(jnp.float32) * back_proj, axis=1).astype(jnp.bfloat16)
    scaled = slot_gates * back_proj
    d_gate = (scaled * pre_up * sigmoid_gate * (1.0 + pre_gate * (1.0 - sigmoid_gate))).astype(
        jnp.bfloat16
    )
    d_up = (scaled * activation).astype(jnp.bfloat16)
    hidden_gated = (slot_gates * hidden.astype(jnp.float32)).astype(jnp.bfloat16)
    partial_value = (
        jnp.einsum("rh,dh->rd", d_gate, relaid[0], preferred_element_type=jnp.float32)
        + jnp.einsum("rh,dh->rd", d_up, relaid[1], preferred_element_type=jnp.float32)
    ).astype(jnp.bfloat16)
    grad_gate = jnp.einsum("rd,rh->dh", slot_tokens, d_gate, preferred_element_type=jnp.float32)
    grad_up = jnp.einsum("rd,rh->dh", slot_tokens, d_up, preferred_element_type=jnp.float32)
    grad_down = jnp.einsum(
        "rd,rh->dh", slot_cotan, hidden_gated, preferred_element_type=jnp.float32
    )
    rows = groups * CAP
    back_parts = lax.all_to_all(
        partial_value.reshape(slabs, rows, part), "expert", split_axis=0, concat_axis=0, tiled=True
    )
    back_scores = lax.all_to_all(
        score_part.reshape(slabs, rows), "expert", split_axis=0, concat_axis=0, tiled=True
    )
    part_sum = jnp.sum(
        back_parts.reshape(experts, HSPLIT, groups, CAP, part).astype(jnp.float32), axis=1
    ).astype(jnp.bfloat16)
    part_sum = lax.all_to_all(
        jnp.moveaxis(part_sum, 1, 0), "dp", split_axis=0, concat_axis=3, tiled=True
    ).reshape(slot_total, features)
    own = lax.axis_index("dp")
    score_sum = jnp.sum(
        back_scores.reshape(experts, HSPLIT, groups, CAP).astype(jnp.float32), axis=1
    )
    score_sum = lax.dynamic_index_in_dim(score_sum, own, 1, keepdims=False).reshape(slot_total)
    token_grad = jnp.einsum(
        "tc,cd->td", pick_half, part_sum, preferred_element_type=jnp.float32
    ).astype(jnp.bfloat16)
    gate_grad = jnp.einsum(
        "tkc,c->tk", select.astype(jnp.float32), score_sum, precision=lax.Precision.HIGHEST
    )
    return (
        relaid[0:1],
        relaid[1:2],
        relaid[2:3],
        grad_gate[None],
        grad_up[None],
        grad_down[None],
        token_grad,
        gate_grad,
    )


def solution(mesh):
    in_specs = (
        P(("dp", "expert"), None),
        P(("dp", "expert"), None),
        P(("dp", "expert"), None),
        P(("dp", "expert"), None),
        P("expert", None, "dp"),
        P("expert", None, "dp"),
        P("expert", None, "dp"),
    )
    out_specs = (
        P("expert", "dp", None),
        P("expert", "dp", None),
        P("expert", "dp", None),
        P("expert", "dp", None),
        P("expert", "dp", None),
        P("expert", "dp", None),
        P(("dp", "expert"), None),
        P(("dp", "expert"), None),
    )
    fits = mesh.shape["dp"] == 2 and mesh.shape["expert"] == HSPLIT
    body = one_expert if fits else shards
    return jax.shard_map(body, mesh=mesh, in_specs=in_specs, out_specs=out_specs, check_vma=False)
```

```python
import jax
import jax.numpy as jnp
from jax import lax
from jax.experimental import pallas as pl
from jax.experimental.pallas import tpu as pltpu
from jax.sharding import PartitionSpec as P

HSPLIT = 16
CAP = 6


MESH_ID = pl.DeviceIdType.MESH
LANES = 128
CHIPS = 8
Y_SLOTS, Y_GATE, Y_UP, Y_DOWN, Y_PRE, Y_SUM, Y_BACK = range(7)
Z0, X0, C0, SIB, RX0, RZ0, COPIES = 6, 10, 14, 22, 23, 26, 30


def dot(left, right, left_dim, right_dim):
    return lax.dot_general(
        left, right, (((left_dim,), (right_dim,)), ((), ())), preferred_element_type=jnp.float32
    )


def exchange_kernel(
    tok_ref,
    cot_ref,
    ids_ref,
    gates_ref,
    wg_ref,
    wu_ref,
    wd_ref,
    relaid_gate_out,
    relaid_up_out,
    relaid_down_out,
    grad_gate_out,
    grad_up_out,
    grad_down_out,
    token_grad_out,
    gate_grad_ref,
    slot_send,
    slot_recv,
    blocks,
    w2,
    w3,
    pre_send,
    pre_recv,
    hid,
    hid_core,
    parts,
    sib_parts,
    x_send,
    x_recv,
    z_send,
    z_recv,
    sum_send,
    sum_recv,
    tok_vmem,
    cot_vmem,
    relaid_gate_ref,
    relaid_up_ref,
    relaid_down_ref,
    grad_gate_ref,
    grad_up_ref,
    grad_down_ref,
    token_grad_ref,
    send_sems,
    recv_sems,
    local_sems,
):
    dp = lax.axis_index("dp")
    me = lax.axis_index("expert")
    half = w2.shape[1]
    wide = half + LANES
    core, chip = lax.rem(me, 2), lax.div(me, 2)
    side, lane = lax.rem(chip, 2), lax.div(chip, 2)

    def member(zz, xx, cc):
        return (zz * 2 + xx) * 2 + cc

    def z_at(step):
        return lax.rem(lane + step + 4, 4)

    partner = (1 - dp, me)
    sibling = (dp, member(lane, side, 1 - core))
    x_other = (dp, member(lane, 1 - side, core))

    def chip_at(step):
        return (dp, lax.rem(chip + step, CHIPS) * 2 + core)

    barrier = pltpu.get_barrier_semaphore()
    for other in [partner, sibling] + [chip_at(k) for k in range(1, CHIPS)]:
        pl.semaphore_signal(barrier, inc=1, device_id=other, device_id_type=MESH_ID)

    def copy(src, dst, number, device):
        out = pltpu.make_async_remote_copy(
            src_ref=src,
            dst_ref=dst,
            send_sem=send_sems.at[number],
            recv_sem=recv_sems.at[number],
            device_id=device,
            device_id_type=MESH_ID,
        )
        return out

    other_cols = pl.ds(pl.multiple_of((1 - dp) * half, LANES), half)
    own_cols = pl.ds(pl.multiple_of(dp * half, LANES), half)
    units = wg_ref.shape[0]
    rows_g = pl.ds(pl.multiple_of(dp * units, 64), units)
    rows_u = pl.ds(pl.multiple_of(2 * units + dp * units, 64), units)
    local = [
        pltpu.make_async_copy(source, target, local_sems.at[number])
        for number, (source, target) in enumerate(
            [
                (tok_ref, tok_vmem),
                (cot_ref, cot_vmem),
                (wg_ref.at[:, own_cols], w2.at[rows_g, :]),
                (wu_ref.at[:, own_cols], w2.at[rows_u, :]),
                (wd_ref.at[:, own_cols], w3.at[rows_g, :]),
            ]
        )
    ]
    for out in local:
        out.start()

    def store(number, source, target):
        out = pltpu.make_async_copy(source, target, local_sems.at[5 + number])
        out.start()
        return out

    tok_count = ids_ref.shape[1]
    hits = (ids_ref[...] == 0).astype(jnp.float32)
    hit = jnp.sum(hits, axis=0, keepdims=True)
    earlier = (
        lax.broadcasted_iota(jnp.int32, (tok_count, tok_count), 0)
        < lax.broadcasted_iota(jnp.int32, (tok_count, tok_count), 1)
    ).astype(jnp.bfloat16)
    rank = dot(jnp.broadcast_to(hit, (16, tok_count)).astype(jnp.bfloat16), earlier, 1, 0)
    row = lax.broadcasted_iota(jnp.int32, (16, tok_count), 0)
    slot = rank.astype(jnp.int32)
    named = jnp.broadcast_to(hit, (16, tok_count))

    def placed(first):
        return jnp.where(row == slot + first, named, 0.0)

    pick = placed(0)
    gate_of = jnp.sum(hits * gates_ref[...].astype(jnp.float32), axis=0, keepdims=True)
    slot_gate = jnp.sum(pick * gate_of, axis=1, keepdims=True)
    pick_tok = pick.astype(jnp.bfloat16)
    pick_cot = placed(8).astype(jnp.bfloat16)

    def slots_of(which):
        cols = pl.ds(pl.multiple_of(which * half, LANES), half)
        return dot(pick_tok, tok_vmem[:, cols], 1, 0) + dot(pick_cot, cot_vmem[:, cols], 1, 0)

    y_gate = copy(wg_ref.at[:, other_cols], w2.at[rows_g, :], Y_GATE, partner)
    y_up = copy(wu_ref.at[:, other_cols], w2.at[rows_u, :], Y_UP, partner)
    y_down = copy(wd_ref.at[:, other_cols], w3.at[rows_g, :], Y_DOWN, partner)
    pl.semaphore_wait(barrier, CHIPS + 1)
    y_gate.start()
    local[0].wait()
    local[1].wait()
    gate_lanes = jnp.broadcast_to(slot_gate, (16, LANES))
    slot_send[:, :half] = slots_of(1 - dp).astype(jnp.bfloat16)
    slot_send[:, half:] = gate_lanes.astype(jnp.bfloat16)
    y_slots = copy(slot_send, slot_recv, Y_SLOTS, partner)
    y_slots.start()
    y_up.start()
    y_down.start()

    own = slots_of(dp)
    own = jnp.concatenate([own, gate_lanes], axis=1)
    y_slots.wait_recv()
    got = slot_recv[...].astype(jnp.float32)
    low = jnp.where(dp == 0, own, got)
    high = jnp.where(dp == 0, got, own)
    blocks[me, 0:16, :] = jnp.concatenate([low[0:8], high[0:8]], axis=0).astype(jnp.bfloat16)
    blocks[me, 16:32, :] = jnp.concatenate([low[8:16], high[8:16]], axis=0).astype(jnp.bfloat16)

    def send_block(source, number, device):
        out = copy(blocks.at[source], blocks.at[source], number, device)
        out.start()
        return out

    gathered = []
    along_z = [send_block(me, Z0 + k, (dp, member(z_at(k), side, core))) for k in range(1, 4)]
    along_x = [send_block(me, X0, x_other)]
    on_chip = [send_block(me, C0, sibling)]
    for k in range(1, 4):
        along_z[k - 1].wait_recv()
        source = member(z_at(-k), side, core)
        along_x.append(send_block(source, X0 + k, x_other))
        on_chip.append(send_block(source, C0 + 2 * k, sibling))
    for k in range(4):
        along_x[k].wait_recv()
        source = member(z_at(-k), 1 - side, core)
        on_chip.append(send_block(source, C0 + 2 * k + 1, sibling))
    for out in on_chip:
        out.wait_recv()
    gathered = along_z + along_x + on_chip

    total = blocks.shape[0] * 16
    slot_tok = blocks[:, 0:16, 0:half].reshape(total, half)
    slot_cot = blocks[:, 16:32, 0:half].reshape(total, half)
    slot_gates = blocks[:, 0:16, half:wide].reshape(total, LANES).astype(jnp.float32)
    for out in local[2:]:
        out.wait()
    y_gate.wait_recv()
    y_up.wait_recv()
    pre = dot(slot_tok, w2[...], 1, 1)
    fore, aft = pl.ds(0, 2 * LANES), pl.ds(2 * LANES, LANES)
    pre_send[:, fore] = pre.astype(jnp.bfloat16)
    y_pre = copy(pre_send.at[:, fore], pre_recv.at[:, fore], Y_PRE, partner)
    y_pre.start()
    relaid_gate_ref[...] = jnp.transpose(w2[0:LANES, :])
    relaid_up_ref[...] = jnp.transpose(w2[LANES:, :])
    y_down.wait_recv()
    back = dot(slot_cot, w3[...], 1, 1)
    pre_send[:, aft] = back.astype(jnp.bfloat16)
    y_back = copy(pre_send.at[:, aft], pre_recv.at[:, aft], Y_BACK, partner)
    y_back.start()
    relaid_down_ref[...] = jnp.transpose(w3[...])
    stores = [
        store(0, relaid_gate_ref, relaid_gate_out),
        store(1, relaid_up_ref, relaid_up_out),
        store(2, relaid_down_ref, relaid_down_out),
    ]
    y_pre.wait_recv()
    y_back.wait_recv()
    pre_gate = pre[:, :LANES] + pre_recv[:, :LANES].astype(jnp.float32)
    pre_up = pre[:, LANES:] + pre_recv[:, LANES : 2 * LANES].astype(jnp.float32)
    back_proj = back + pre_recv[:, 2 * LANES :].astype(jnp.float32)
    sig = jax.nn.sigmoid(pre_gate)
    activation = pre_gate * sig
    hidden = (activation * pre_up).astype(jnp.bfloat16).astype(jnp.float32)
    score = jnp.sum(hidden * back_proj, axis=1, keepdims=True)
    scaled = slot_gates * back_proj
    d_gate = (scaled * pre_up * sig * (1.0 + pre_gate * (1.0 - sig))).astype(jnp.bfloat16)
    d_up = (scaled * activation).astype(jnp.bfloat16)
    by_core = jnp.concatenate([d_gate, d_up], axis=1)
    hid[:, : 2 * LANES] = by_core
    hid[:, 2 * LANES :] = (slot_gates * hidden).astype(jnp.bfloat16)
    by_core = by_core.reshape(CHIPS, 2, 16, 2 * LANES)
    hid_core[0] = by_core[:, 0].reshape(total // 2, 2 * LANES)
    hid_core[1] = by_core[:, 1].reshape(total // 2, 2 * LANES)
    scores = jnp.broadcast_to(score, (total, LANES)).astype(jnp.bfloat16)
    scores = scores.reshape(CHIPS, 2, 16, LANES)
    parts[0, :, :, half:] = scores[:, 0]
    parts[1, :, :, half:] = scores[:, 1]

    def put_parts(to):
        for tile in range(half // 256):
            cols = pl.ds(tile * 256, 256)
            value = dot(hid_core[to], w2[:, cols], 1, 0).astype(jnp.bfloat16)
            parts[to, :, :, cols] = value.reshape(CHIPS, 16, 256)

    put_parts(1 - core)
    to_sibling = copy(parts.at[1 - core], sib_parts, SIB, sibling)
    to_sibling.start()
    put_parts(core)

    def grads(first, last):
        @pl.loop(first, last)
        def _(tile):
            cols = pl.ds(pl.multiple_of(tile * 256, 256), 256)
            x_tile = blocks[:, 0:16, cols].reshape(total, 256)
            y_tile = blocks[:, 16:32, cols].reshape(total, 256)
            both = dot(x_tile, hid[:, : 2 * LANES], 0, 0)
            grad_gate_ref[cols, :] = both[:, :LANES]
            grad_up_ref[cols, :] = both[:, LANES:]
            grad_down_ref[cols, :] = dot(y_tile, hid[:, 2 * LANES :], 0, 0)

    grads(0, 1)
    to_sibling.wait_recv()
    def chip_sum(dest):
        return parts[core, dest].astype(jnp.float32) + sib_parts[dest].astype(jnp.float32)

    returned, across_x, back_z = [], {}, []
    order = (2, 1, 3, 0)
    for k in order:
        x_send[k] = chip_sum(z_at(k) * 2 + 1 - side).astype(jnp.bfloat16)
        across_x[k] = copy(x_send.at[k], x_recv.at[k], RX0 + k, x_other)
        across_x[k].start()
        returned.append(across_x[k])
    for k in order:
        across_x[k].wait_recv()
        own_sum = chip_sum(z_at(k) * 2 + side) + x_recv[k].astype(jnp.float32)
        if k:
            z_send[k] = own_sum.astype(jnp.bfloat16)
            out = copy(z_send.at[k], z_recv.at[k], RZ0 + k, (dp, member(z_at(k), side, core)))
            out.start()
            back_z.append((k, out))
            returned.append(out)
    grads(1, half // 256)
    stores += [
        store(3, grad_gate_ref, grad_gate_out),
        store(4, grad_up_ref, grad_up_out),
        store(5, grad_down_ref, grad_down_out),
    ]
    for k, out in back_z:
        out.wait_recv()
        own_sum = own_sum + z_recv[k].astype(jnp.float32)
    sum_send[...] = own_sum[:, :half].astype(jnp.bfloat16)
    y_sum = copy(sum_send, sum_recv, Y_SUM, partner)
    y_sum.start()
    pick_mine = placed(8 * dp)
    score_of = jnp.sum(pick_mine * own_sum[:, half:], axis=0, keepdims=True)
    gate_grad_ref[...] = hits * score_of
    pick_half = pick_mine.astype(jnp.bfloat16)
    token_grad_ref[:, own_cols] = dot(pick_half, sum_send[...], 0, 0).astype(jnp.bfloat16)
    y_sum.wait_recv()
    token_grad_ref[:, other_cols] = dot(pick_half, sum_recv[...], 0, 0).astype(jnp.bfloat16)
    stores.append(store(6, token_grad_ref, token_grad_out))
    for out in stores:
        out.wait()
    for out in [y_slots, y_gate, y_up, y_down, y_pre, y_back, y_sum, to_sibling] + gathered + returned:
        out.wait_send()


def store_kernel(*refs):
    count = len(refs) // 3
    sources, targets, staged = refs[:count], refs[count : 2 * count], refs[2 * count : 3 * count]
    load_sems, store_sems = refs[3 * count :]
    loads = [
        pltpu.make_async_copy(sources[i], staged[i], load_sems.at[i]) for i in range(count)
    ]
    stores = [
        pltpu.make_async_copy(staged[i], targets[i], store_sems.at[i]) for i in range(count)
    ]
    for out in loads:
        out.start()
    for i in range(count):
        loads[i].wait()
        stores[i].start()
    for out in stores:
        out.wait()


def one_expert(tokens, cotangent, route_ids, gates, w_gate, w_up, w_down):
    slabs = lax.axis_size("expert")
    tok_count, features = tokens.shape
    top_count = route_ids.shape[1]
    half = features // 2
    wide = half + LANES
    total = slabs * 16
    bf16, f32 = jnp.bfloat16, jnp.float32
    vmem = pl.BlockSpec(memory_space=pltpu.VMEM)
    hbm = pl.BlockSpec(memory_space=pltpu.HBM)
    outs = pl.pallas_call(
        exchange_kernel,
        out_shape=[jax.ShapeDtypeStruct((half, LANES), bf16)] * 3
        + [jax.ShapeDtypeStruct((half, LANES), f32)] * 3
        + [
            jax.ShapeDtypeStruct((tok_count, features), bf16),
            jax.ShapeDtypeStruct((top_count, tok_count), f32),
        ],
        in_specs=[hbm, hbm, vmem, vmem, hbm, hbm, hbm],
        out_specs=[hbm] * 7 + [vmem],
        scratch_shapes=[
            pltpu.VMEM((16, wide), bf16),
            pltpu.VMEM((16, wide), bf16),
            pltpu.VMEM((slabs, 32, wide), bf16),
            pltpu.VMEM((2 * LANES, half), bf16),
            pltpu.VMEM((LANES, half), bf16),
            pltpu.VMEM((total, 3 * LANES), bf16),
            pltpu.VMEM((total, 3 * LANES), bf16),
            pltpu.VMEM((total, 3 * LANES), bf16),
            pltpu.VMEM((2, total // 2, 2 * LANES), bf16),
            pltpu.VMEM((2, CHIPS, 16, wide), bf16),
            pltpu.VMEM((CHIPS, 16, wide), bf16),
            pltpu.VMEM((4, 16, wide), bf16),
            pltpu.VMEM((4, 16, wide), bf16),
            pltpu.VMEM((4, 16, wide), bf16),
            pltpu.VMEM((4, 16, wide), bf16),
            pltpu.VMEM((16, half), bf16),
            pltpu.VMEM((16, half), bf16),
            pltpu.VMEM((tok_count, features), bf16),
            pltpu.VMEM((tok_count, features), bf16),
            pltpu.VMEM((half, LANES), bf16),
            pltpu.VMEM((half, LANES), bf16),
            pltpu.VMEM((half, LANES), bf16),
            pltpu.VMEM((half, LANES), f32),
            pltpu.VMEM((half, LANES), f32),
            pltpu.VMEM((half, LANES), f32),
            pltpu.VMEM((tok_count, features), bf16),
            pltpu.SemaphoreType.DMA((COPIES,)),
            pltpu.SemaphoreType.DMA((COPIES,)),
            pltpu.SemaphoreType.DMA((12,)),
        ],
        compiler_params=pltpu.CompilerParams(
            collective_id=0, has_side_effects=True, vmem_limit_bytes=58 * 2**20
        ),
        cost_estimate=pl.CostEstimate(
            flops=16 * total * half * LANES, bytes_accessed=12 * 2**20, transcendentals=total * LANES
        ),
    )(
        tokens,
        cotangent,
        route_ids.T,
        gates.T,
        w_gate[0].T,
        w_up[0].T,
        w_down[0].T,
    )
    outs = pl.pallas_call(
        store_kernel,
        out_shape=[jax.ShapeDtypeStruct(value.shape, value.dtype) for value in outs],
        in_specs=[hbm] * 8,
        out_specs=[hbm] * 8,
        scratch_shapes=[pltpu.VMEM(value.shape, value.dtype) for value in outs]
        + [pltpu.SemaphoreType.DMA((8,))] * 2,
        compiler_params=pltpu.CompilerParams(vmem_limit_bytes=58 * 2**20),
        cost_estimate=pl.CostEstimate(flops=0, bytes_accessed=10 * 2**20, transcendentals=0),
    )(*outs)
    return tuple(value[None] for value in outs[:6]) + (outs[6], outs[7].T)


def shards(tokens, cotangent, route_ids, gates, w_gate, w_up, w_down):
    slabs = lax.axis_size("expert")
    groups = lax.axis_size("dp")
    experts = slabs // HSPLIT
    tok_count, features = tokens.shape
    part = features // groups
    top_count = route_ids.shape[1]
    slot_total = experts * CAP
    flat_ids = route_ids.reshape(-1)
    expert_hits = (flat_ids[:, None] == jnp.arange(experts, dtype=jnp.int32)[None, :]).astype(
        jnp.int32
    )
    earlier = jnp.cumsum(expert_hits, axis=0) - expert_hits
    slot_rank = jnp.sum(earlier * expert_hits, axis=1)
    in_slab = jnp.sum(expert_hits, axis=1) > 0
    slot_index = flat_ids * CAP + slot_rank
    table = (slot_index[:, None] == jnp.arange(slot_total, dtype=jnp.int32)[None, :]) & in_slab[
        :, None
    ]
    select = table.reshape(tok_count, top_count, slot_total)
    picked = jnp.any(select, axis=1)
    pick_half = picked.astype(jnp.bfloat16)
    token_slots = jnp.einsum(
        "tc,td->cd", pick_half, tokens, preferred_element_type=jnp.float32
    ).astype(jnp.bfloat16)
    cotan_slots = jnp.einsum(
        "tc,td->cd", pick_half, cotangent, preferred_element_type=jnp.float32
    ).astype(jnp.bfloat16)
    gate_slots = jnp.sum(
        jnp.where(select, gates[:, :, None].astype(jnp.float32), 0.0), axis=(0, 1)
    ).astype(jnp.bfloat16)
    weights = jnp.stack([w_gate[0], w_up[0], w_down[0]])
    relaid = lax.all_to_all(weights, "dp", split_axis=1, concat_axis=2, tiled=True)
    both = jnp.stack([token_slots, cotan_slots]).reshape(2, experts, CAP, groups, part)
    both = jnp.moveaxis(both, 3, 0)
    both = lax.all_to_all(both, "dp", split_axis=0, concat_axis=0, tiled=True)
    gate_all = lax.all_gather(gate_slots.reshape(experts, CAP), "dp", axis=0, tiled=False)
    if experts == 1:
        recv = lax.all_gather(both, "expert", axis=0, tiled=False)[:, :, :, 0]
        gate_recv = lax.all_gather(gate_all, "expert", axis=0, tiled=False)[:, :, 0]
    else:
        send = jnp.repeat(jnp.moveaxis(both, 2, 0), HSPLIT, axis=0)
        recv = lax.all_to_all(send, "expert", split_axis=0, concat_axis=0, tiled=True)
        gate_send = jnp.repeat(jnp.moveaxis(gate_all, 1, 0), HSPLIT, axis=0)
        gate_recv = lax.all_to_all(gate_send, "expert", split_axis=0, concat_axis=0, tiled=True)
    slot_tokens = recv[:, :, 0].reshape(-1, part)
    slot_cotan = recv[:, :, 1].reshape(-1, part)
    slot_gates = gate_recv.reshape(-1).astype(jnp.float32)[:, None]
    pre_part = jnp.stack(
        [
            jnp.dot(slot_tokens, relaid[0], preferred_element_type=jnp.float32),
            jnp.dot(slot_tokens, relaid[1], preferred_element_type=jnp.float32),
            jnp.dot(slot_cotan, relaid[2], preferred_element_type=jnp.float32),
        ]
    )
    pre_gate, pre_up, back_proj = lax.psum(pre_part, "dp")
    sigmoid_gate = jax.nn.sigmoid(pre_gate)
    activation = pre_gate * sigmoid_gate
    hidden = (activation * pre_up).astype(jnp.bfloat16)
    score_part = jnp.sum(hidden.astype(jnp.float32) * back_proj, axis=1).astype(jnp.bfloat16)
    scaled = slot_gates * back_proj
    d_gate = (scaled * pre_up * sigmoid_gate * (1.0 + pre_gate * (1.0 - sigmoid_gate))).astype(
        jnp.bfloat16
    )
    d_up = (scaled * activation).astype(jnp.bfloat16)
    hidden_gated = (slot_gates * hidden.astype(jnp.float32)).astype(jnp.bfloat16)
    partial_value = (
        jnp.einsum("rh,dh->rd", d_gate, relaid[0], preferred_element_type=jnp.float32)
        + jnp.einsum("rh,dh->rd", d_up, relaid[1], preferred_element_type=jnp.float32)
    ).astype(jnp.bfloat16)
    grad_gate = jnp.einsum("rd,rh->dh", slot_tokens, d_gate, preferred_element_type=jnp.float32)
    grad_up = jnp.einsum("rd,rh->dh", slot_tokens, d_up, preferred_element_type=jnp.float32)
    grad_down = jnp.einsum(
        "rd,rh->dh", slot_cotan, hidden_gated, preferred_element_type=jnp.float32
    )
    rows = groups * CAP
    back_parts = lax.all_to_all(
        partial_value.reshape(slabs, rows, part), "expert", split_axis=0, concat_axis=0, tiled=True
    )
    back_scores = lax.all_to_all(
        score_part.reshape(slabs, rows), "expert", split_axis=0, concat_axis=0, tiled=True
    )
    part_sum = jnp.sum(
        back_parts.reshape(experts, HSPLIT, groups, CAP, part).astype(jnp.float32), axis=1
    ).astype(jnp.bfloat16)
    part_sum = lax.all_to_all(
        jnp.moveaxis(part_sum, 1, 0), "dp", split_axis=0, concat_axis=3, tiled=True
    ).reshape(slot_total, features)
    own = lax.axis_index("dp")
    score_sum = jnp.sum(
        back_scores.reshape(experts, HSPLIT, groups, CAP).astype(jnp.float32), axis=1
    )
    score_sum = lax.dynamic_index_in_dim(score_sum, own, 1, keepdims=False).reshape(slot_total)
    token_grad = jnp.einsum(
        "tc,cd->td", pick_half, part_sum, preferred_element_type=jnp.float32
    ).astype(jnp.bfloat16)
    gate_grad = jnp.einsum(
        "tkc,c->tk", select.astype(jnp.float32), score_sum, precision=lax.Precision.HIGHEST
    )
    return (
        relaid[0:1],
        relaid[1:2],
        relaid[2:3],
        grad_gate[None],
        grad_up[None],
        grad_down[None],
        token_grad,
        gate_grad,
    )


def solution(mesh):
    in_specs = (
        P(("dp", "expert"), None),
        P(("dp", "expert"), None),
        P(("dp", "expert"), None),
        P(("dp", "expert"), None),
        P("expert", None, "dp"),
        P("expert", None, "dp"),
        P("expert", None, "dp"),
    )
    out_specs = (
        P("expert", "dp", None),
        P("expert", "dp", None),
        P("expert", "dp", None),
        P("expert", "dp", None),
        P("expert", "dp", None),
        P("expert", "dp", None),
        P(("dp", "expert"), None),
        P(("dp", "expert"), None),
    )
    fits = mesh.shape["dp"] == 2 and mesh.shape["expert"] == HSPLIT
    body = one_expert if fits else shards
    return jax.shard_map(body, mesh=mesh, in_specs=in_specs, out_specs=out_specs, check_vma=False)
```
